256 devices in a mesh: tile: 64 (over y, z, core), panel: 4 (over x).
Axes of the slice: x: 4, y: 4, z: 8, core: 2. Of those that a mesh axis runs over, the one named last changes fastest.
Arguments:
- wavefield: bfloat16 [2, 16384, 64], P(None, ('tile', 'panel')), may hold values from -6 to 6
- residual: bfloat16 [2, 16384, 64], P(None, ('tile', 'panel')), may hold values from -6 to 6
- v_factors: bfloat16 [64, 64, 2, 256, 128], P(None, 'tile', None, 'panel'), may hold values from -0.375 to 0.375
- u_factors: bfloat16 [64, 64, 2, 256, 128], P('tile', None, None, 'panel'), may hold values from -0.09375 to 0.09375
- tile_ranks: int32 [64, 64], replicated, may hold values from 1 to 128
- tile_present: int32 [64, 64], replicated, may hold values 0 or 1
Outputs:
- predicted: bfloat16 [2, 16384, 64], P(None, ('tile', 'panel'))
- gradient: bfloat16 [2, 16384, 64], P(None, ('tile', 'panel'))
The draws below stay inside these ranges and needn't reach their ends.
All inputs are finite; a program needn't handle non-finite values.
Results may differ from the reference program's by a relative error of at most 0.018.
Values may be sent and summed in bfloat16 or wider, within the bound.
A program may use at most 64 MiB of HBM per device.

```python
import jax
import jax.numpy as jnp
from jax import lax

TILE = 256
RMAX = 128
SRC = 64
NT = 64
N = 16384
N_PANEL = 4


def plant(result, key, low, largest):
    longest = result.shape.index(max(result.shape))
    spots = []
    for shift in (0, 1):
        where = [jax.random.randint(jax.random.fold_in(key, axis), (), 0, length) for axis, length in enumerate(result.shape)]
        where[longest] = (where[longest] + shift) % result.shape[longest]
        spots.append(tuple(where))
    return result.at[spots[0]].set(low).at[spots[1]].set(largest)


def block_levels(stream_key, extent, split, least, largest):
    loudness, own = 1.0, jax.random.fold_in(stream_key, 6)
    for position, shards_of in split:
        heights = jnp.exp(jax.random.uniform(jax.random.fold_in(own, position), (shards_of,), jnp.float32, least / len(split), largest / len(split)))
        loudness = loudness * jnp.repeat(heights, extent[position] // shards_of).reshape([-1 if axis == position else 1 for axis in range(len(extent))])
    return loudness


def gaussian(key, dims, width, most, pieces=(), held_as=jnp.bfloat16):
    drawn = jax.random.normal(key, dims, jnp.float32) * width
    if len(pieces) > 0:
        drawn = block_levels(key, dims, pieces, -0.22, 0.18) * drawn
    return jnp.clip(drawn, min=-most, max=most).astype(held_as)


def setup_inputs(seed: int = 0) -> dict:
    streams_of = jax.random.split(jax.random.key(seed), 7)
    wavefield = gaussian(streams_of[0], (2, N, SRC), 1.0, 6.0, ((1, 256),))
    residual = gaussian(streams_of[1], (2, N, SRC), 1.0, 6.0, ((1, 256),))
    v_factors = gaussian(streams_of[2], (NT, NT, 2, TILE, RMAX), TILE ** -0.5, 0.375, ((1, 64), (3, 4)))
    u_factors = gaussian(streams_of[3], (NT, NT, 2, TILE, RMAX), (NT * RMAX // 2) ** -0.5, 0.09375, ((0, 64), (3, 4)))
    tile_ranks = plant(jax.random.randint(streams_of[4], (NT, NT), 1, RMAX + 1), jax.random.fold_in(streams_of[4], 1), 1, RMAX).astype(jnp.int32)
    tile_present = plant((jax.random.randint(streams_of[5], (NT, NT), 0, 4) < 3).astype(jnp.int32), jax.random.fold_in(streams_of[5], 1), 0, 1)
    return dict(wavefield=wavefield, residual=residual, v_factors=v_factors, u_factors=u_factors, tile_ranks=tile_ranks, tile_present=tile_present)


def conj_product(factor, vector, weight):
    prows = TILE // N_PANEL
    fac = factor.astype(jnp.float32).reshape(NT, 2, N_PANEL, prows, RMAX)
    vec = vector.astype(jnp.float32).reshape(2, N_PANEL, prows, SRC)
    real_a = jnp.einsum('nprk,prs->npsk', fac[:, 0], vec[0])
    real_b = jnp.einsum('nprk,prs->npsk', fac[:, 1], vec[1])
    imag_a = jnp.einsum('nprk,prs->npsk', fac[:, 0], vec[1])
    imag_b = jnp.einsum('nprk,prs->npsk', fac[:, 1], vec[0])
    parts = jnp.stack([real_a + real_b, imag_a - imag_b], axis=2)
    parts = parts * weight[:, None, None, None, :]
    parts = parts.astype(jnp.bfloat16).astype(jnp.float32)
    return jnp.sum(parts, axis=1).astype(jnp.bfloat16)


def out_product(factor, space):
    fac = factor.astype(jnp.float32)
    spc = space.astype(jnp.float32)
    first = jnp.einsum('nrk,ncsk->crs', fac[:, 0], spc)
    second = jnp.einsum('nrk,ncsk->crs', fac[:, 1], spc)
    real_part = first[0] - second[1]
    imag_part = first[1] + second[0]
    return jnp.stack([real_part, imag_part], axis=0).astype(jnp.bfloat16)


def reference(wavefield, residual, v_factors, u_factors, tile_ranks, tile_present):
    levels = jnp.arange(RMAX, dtype=jnp.int32)
    indices = jnp.arange(NT, dtype=jnp.int32)

    def weights(rank_row, present_row):
        keep = (levels[None, :] < rank_row[:, None]) & (present_row[:, None] == 1)
        return keep.astype(jnp.float32)

    def column(colidx):
        weight = weights(tile_ranks[:, colidx], tile_present[:, colidx])
        rows = lax.dynamic_slice_in_dim(wavefield, (colidx * TILE).astype(jnp.int32), TILE, 1)
        return conj_product(v_factors[:, colidx], rows, weight)

    fspace = lax.map(column, indices)

    def row_out(rowidx):
        return out_product(u_factors[rowidx], fspace[:, rowidx])

    predicted = lax.map(row_out, indices)
    predicted = jnp.transpose(predicted, (1, 0, 2, 3)).reshape(2, NT * TILE, SRC)

    def row_in(rowidx):
        weight = weights(tile_ranks[rowidx, :], tile_present[rowidx, :])
        rows = lax.dynamic_slice_in_dim(residual, (rowidx * TILE).astype(jnp.int32), TILE, 1)
        return conj_product(u_factors[rowidx], rows, weight)

    aspace = lax.map(row_in, indices)

    def column_out(colidx):
        return out_product(v_factors[:, colidx], aspace[:, colidx])

    gradient = lax.map(column_out, indices)
    gradient = jnp.transpose(gradient, (1, 0, 2, 3)).reshape(2, NT * TILE, SRC)
    return predicted, gradient
```

```python
import functools

import jax
import jax.numpy as jnp
from jax import lax
from jax.experimental import pallas as pl
from jax.experimental.pallas import tpu as pltpu
from jax.sharding import PartitionSpec as P

MESH = pl.DeviceIdType.MESH
PANELS = 4
V_CHUNKS = (4, 4, 4, 4)
U_CHUNKS = (4, 4, 4, 2, 1, 1)


def spans(sizes):
    starts = []
    at = 0
    for size in sizes:
        starts.append((at, size))
        at += size
    return starts


def kernel(
    groups,
    wave_hbm, resid_hbm, v_hbm, u_hbm, rank_hbm, present_hbm,
    pred_ref, grad_ref,
    raw, joined, vec_w, vec_r, v_all, u_all, f_send, f_recv, a_send, a_recv,
    acc_p, acc_g, own_sum, part_send, part_recv, ranks, present,
    raw_sem, rank_sem, own_sem, x_send, x_recv, v_ssem, v_rsem, u_ssem, u_rsem,
    f_ssem, f_rsem, a_ssem, a_rsem, p_ssem, p_rsem,
):
    t = lax.axis_index("tile")
    p = lax.axis_index("panel")
    me = t // PANELS
    low = t % PANELS
    q = (p + PANELS - low) % PANELS
    alone = q == low

    raw_copies = [
        pltpu.make_async_copy(wave_hbm, raw.at[0], raw_sem.at[0]),
        pltpu.make_async_copy(resid_hbm, raw.at[1], raw_sem.at[1]),
    ]
    rank_copies = [
        pltpu.make_async_copy(rank_hbm, ranks, rank_sem.at[0]),
        pltpu.make_async_copy(present_hbm, present, rank_sem.at[1]),
    ]
    own_copies = [
        pltpu.make_async_copy(v_hbm.at[:, q], v_all.at[:, :, p], own_sem.at[0]),
        pltpu.make_async_copy(u_hbm.at[:, q], u_all.at[:, :, p], own_sem.at[1]),
    ]
    for copy in raw_copies + rank_copies:
        copy.start()

    barrier = pltpu.get_barrier_semaphore()
    for d in (1, 2, 3):
        pl.semaphore_signal(barrier, inc=1, device_id=(t, (p + d) % PANELS), device_id_type=MESH)

    def greet(n, carry):
        other = PANELS * n + q

        @pl.when(other != t)
        def _():
            pl.semaphore_signal(barrier, inc=1, device_id=(other, p), device_id_type=MESH)

        return carry

    lax.fori_loop(0, groups, greet, 0)
    for copy in own_copies:
        copy.start()
    for copy in raw_copies:
        copy.wait()
    for k in (0, 1):
        joined[k, p] = jnp.concatenate([raw[k, 0], raw[k, 1]], axis=1)

    @pl.when(alone)
    def _():
        pl.semaphore_wait(barrier, 3 + groups - 1)

    @pl.when(jnp.logical_not(alone))
    def _():
        pl.semaphore_wait(barrier, 3 + groups)

    def vec_copy(d):
        return pltpu.make_async_remote_copy(
            joined.at[:, p], joined.at[:, p], x_send.at[d - 1], x_recv.at[d - 1],
            device_id=(t, (p + d) % PANELS), device_id_type=MESH,
        )

    def vec_arrival(d):
        source = (p + PANELS - d) % PANELS
        return pltpu.make_async_remote_copy(
            joined.at[:, source], joined.at[:, source], x_send.at[d - 1], x_recv.at[d - 1],
            device_id=(t, source), device_id_type=MESH,
        )

    def factor_copy(src, dst, ssem, rsem, c, start, size, d):
        return pltpu.make_async_remote_copy(
            src.at[pl.ds(start, size), (q + d) % PANELS],
            dst.at[pl.ds(start, size), :, p],
            ssem.at[c, d - 1], rsem.at[c, d - 1],
            device_id=(t, (p + d) % PANELS), device_id_type=MESH,
        )

    def factor_arrival(src, dst, ssem, rsem, c, start, size, d):
        source = (p + PANELS - d) % PANELS
        return pltpu.make_async_remote_copy(
            src.at[pl.ds(start, size), q],
            dst.at[pl.ds(start, size), :, source],
            ssem.at[c, d - 1], rsem.at[c, d - 1],
            device_id=(t, source), device_id_type=MESH,
        )

    for d in (1, 3, 2):
        vec_copy(d).start()
    v_spans = spans(V_CHUNKS)
    u_spans = spans(U_CHUNKS)
    for c, (start, size) in enumerate(v_spans):
        for d in (2, 1, 3):
            factor_copy(v_hbm, v_all, v_ssem, v_rsem, c, start, size, d).start()
    for c, (start, size) in enumerate(u_spans):
        for d in (2, 1, 3):
            factor_copy(u_hbm, u_all, u_ssem, u_rsem, c, start, size, d).start()

    acc_p[...] = jnp.zeros_like(acc_p)
    acc_g[...] = jnp.zeros_like(acc_g)
    for copy in rank_copies:
        copy.wait()
    for d in (1, 3, 2):
        vec_arrival(d).wait_recv()
    for k, vec in ((0, vec_w), (1, vec_r)):
        rows = joined[k].reshape(256, 128).astype(jnp.float32).T
        vec[:, :256] = rows.astype(jnp.bfloat16)
        vec[:, 256:] = jnp.concatenate([rows[64:], -rows[:64]], axis=0).astype(jnp.bfloat16)

    def block_copy(send, recv, ssem, rsem, n):
        return pltpu.make_async_remote_copy(
            send.at[n], recv.at[me], ssem.at[n], rsem.at[me],
            device_id=(PANELS * n + q, p), device_id_type=MESH,
        )

    def block_own(send, recv, rsem, n):
        return pltpu.make_async_copy(send.at[n], recv.at[n], rsem.at[n])

    levels = lax.broadcasted_iota(jnp.int32, (1, 128), 1)

    def project(factor, vec, send, recv, ssem, rsem, start, size, column):
        for n0 in range(start, start + size, 2):
            many = min(2, start + size - n0)
            joint = [factor[n0 + k].reshape(512, 128) for k in range(many)]
            joint = joint[0] if many == 1 else jnp.concatenate(joint, axis=1)
            space = jnp.dot(vec[...], joint, preferred_element_type=jnp.float32)
            for k in range(many):
                n = n0 + k
                other = PANELS * n + q
                if column:
                    rank, here = ranks[other, t], present[other, t]
                else:
                    rank, here = ranks[t, other], present[t, other]
                limit = jnp.where(here == 1, rank, 0)
                part = jnp.where(levels < limit, space[:, 128 * k : 128 * (k + 1)], 0.0)
                send[n] = part.astype(jnp.bfloat16)

                @pl.when(other != t)
                def _():
                    block_copy(send, recv, ssem, rsem, n).start()

                @pl.when(other == t)
                def _():
                    block_own(send, recv, rsem, n).start()

    def expand(factor, recv, rsem, acc, start, size):
        for n0 in range(start, start + size, 2):
            many = min(2, start + size - n0)
            for k in range(many):
                block_own(recv, recv, rsem, n0 + k).wait()
            left = [factor[n0 + k].reshape(512, 128) for k in range(many)]
            right = [recv[n0 + k] for k in range(many)]
            left = left[0] if many == 1 else jnp.concatenate(left, axis=1)
            right = right[0] if many == 1 else jnp.concatenate(right, axis=1)
            acc[...] += lax.dot_general(
                left, right, (((1,), (1,)), ((), ())), preferred_element_type=jnp.float32
            )

    def part_copy(k, d):
        target = (p + d) % PANELS
        return pltpu.make_async_remote_copy(
            part_send.at[k, target], part_recv.at[k, d - 1], p_ssem.at[k, d - 1], p_rsem.at[k, d - 1],
            device_id=(t, target), device_id_type=MESH,
        )

    def send_parts(k, acc):
        lanes = lax.broadcasted_iota(jnp.int32, (256, 128), 1)
        turned = pltpu.roll(acc[256:, :], 64, 1)
        total = acc[:256, :] + jnp.where(lanes < 64, -turned, turned)
        total = total.reshape(PANELS, 64, 128)
        own_sum[k] = total
        part_send[k] = total.astype(jnp.bfloat16)
        for d in (2, 1, 3):
            part_copy(k, d).start()

    def finish(k, out):
        for d in (1, 3, 2):
            part_copy(k, d).wait_recv()
        total = own_sum[k, p]
        for d in (1, 2, 3):
            total = total + part_recv[k, d - 1].astype(jnp.float32)
        out[0] = total[:, :64].astype(jnp.bfloat16)
        out[1] = total[:, 64:].astype(jnp.bfloat16)

    own_copies[0].wait()
    for c, (start, size) in enumerate(v_spans):
        for d in (1, 3, 2):
            factor_arrival(v_hbm, v_all, v_ssem, v_rsem, c, start, size, d).wait_recv()
        project(v_all, vec_w, f_send, f_recv, f_ssem, f_rsem, start, size, True)
    own_copies[1].wait()
    for c, (start, size) in enumerate(u_spans):
        for d in (1, 3, 2):
            factor_arrival(u_hbm, u_all, u_ssem, u_rsem, c, start, size, d).wait_recv()
        project(u_all, vec_r, a_send, a_recv, a_ssem, a_rsem, start, size, False)
        expand(u_all, f_recv, f_rsem, acc_p, start, size)
        if c > 0:
            expand(v_all, a_recv, a_rsem, acc_g, *u_spans[c - 1])
    send_parts(0, acc_p)
    expand(v_all, a_recv, a_rsem, acc_g, *u_spans[-1])
    send_parts(1, acc_g)
    finish(0, pred_ref)
    finish(1, grad_ref)

    for d in (1, 2, 3):
        vec_copy(d).wait_send()
        for c, (start, size) in enumerate(v_spans):
            factor_copy(v_hbm, v_all, v_ssem, v_rsem, c, start, size, d).wait_send()
        for c, (start, size) in enumerate(u_spans):
            factor_copy(u_hbm, u_all, u_ssem, u_rsem, c, start, size, d).wait_send()
        for k in (0, 1):
            part_copy(k, d).wait_send()

    def settle(n, carry):
        @pl.when(PANELS * n + q != t)
        def _():
            block_copy(f_send, f_recv, f_ssem, f_rsem, n).wait_send()
            block_copy(a_send, a_recv, a_ssem, a_rsem, n).wait_send()

        return carry

    lax.fori_loop(0, groups, settle, 0)


def on_device(wavefield, residual, v_factors, u_factors, tile_ranks, tile_present):
    tiles = tile_ranks.shape[0]
    groups = tiles // PANELS
    v_local = v_factors.reshape(groups, PANELS, 2, 64, 128)
    u_local = u_factors.reshape(groups, PANELS, 2, 64, 128)
    hbm = pl.BlockSpec(memory_space=pl.ANY)
    vmem = pl.BlockSpec(memory_space=pltpu.VMEM)
    b16, f32 = jnp.bfloat16, jnp.float32
    dma = pltpu.SemaphoreType.DMA
    result = jax.ShapeDtypeStruct((2, 64, 64), b16)
    pred, grad = pl.pallas_call(
        functools.partial(kernel, groups),
        out_shape=(result, result),
        in_specs=[hbm] * 6,
        out_specs=(vmem, vmem),
        scratch_shapes=[
            pltpu.VMEM((2, 2, 64, 64), b16),
            pltpu.VMEM((2, PANELS, 64, 128), b16),
            pltpu.VMEM((128, 512), b16),
            pltpu.VMEM((128, 512), b16),
            pltpu.VMEM((groups, 2, PANELS, 64, 128), b16),
            pltpu.VMEM((groups, 2, PANELS, 64, 128), b16),
            pltpu.VMEM((groups, 128, 128), b16),
            pltpu.VMEM((groups, 128, 128), b16),
            pltpu.VMEM((groups, 128, 128), b16),
            pltpu.VMEM((groups, 128, 128), b16),
            pltpu.VMEM((512, 128), f32),
            pltpu.VMEM((512, 128), f32),
            pltpu.VMEM((2, PANELS, 64, 128), f32),
            pltpu.VMEM((2, PANELS, 64, 128), b16),
            pltpu.VMEM((2, 3, 64, 128), b16),
            pltpu.SMEM((tiles, tiles), jnp.int32),
            pltpu.SMEM((tiles, tiles), jnp.int32),
            dma((2,)), dma((2,)), dma((2,)),
            dma((3,)), dma((3,)),
            dma((len(V_CHUNKS), 3)), dma((len(V_CHUNKS), 3)),
            dma((len(U_CHUNKS), 3)), dma((len(U_CHUNKS), 3)),
            dma((groups,)), dma((groups,)), dma((groups,)), dma((groups,)),
            dma((2, 3)), dma((2, 3)),
        ],
        compiler_params=pltpu.CompilerParams(
            collective_id=0, has_side_effects=True, vmem_limit_bytes=60 << 20
        ),
        cost_estimate=pl.CostEstimate(flops=1 << 30, bytes_accessed=4 << 20, transcendentals=0),
    )(wavefield, residual, v_local, u_local, tile_ranks, tile_present)
    return pred, grad


def solution(mesh):
    return jax.shard_map(
        on_device,
        mesh=mesh,
        in_specs=(
            P(None, ("tile", "panel"), None),
            P(None, ("tile", "panel"), None),
            P(None, "tile", None, "panel", None),
            P("tile", None, None, "panel", None),
            P(),
            P(),
        ),
        out_specs=(P(None, ("tile", "panel"), None), P(None, ("tile", "panel"), None)),
        check_vma=False,
    )
```

```python
import functools

import jax
import jax.numpy as jnp
from jax import lax
from jax.experimental import pallas as pl
from jax.experimental.pallas import tpu as pltpu
from jax.sharding import PartitionSpec as P

MESH = pl.DeviceIdType.MESH
PANELS = 4
SIDE = 4
FAR_FIRST = (2, 1, 3, 0)
LOOKAHEAD = 4


def column(z):
    return tuple((y, z) for y in FAR_FIRST)


V_CHUNKS = tuple(column(z) for z in FAR_FIRST)
U_CHUNKS = tuple(column(z) for z in FAR_FIRST[:-1]) + tuple((spot,) for spot in column(0))


def opposite(chunk):
    return tuple(((SIDE - y) % SIDE, (SIDE - z) % SIDE) for y, z in chunk)


def kernel(
    groups,
    wave_hbm, resid_hbm, v_hbm, u_hbm, rank_hbm, present_hbm,
    pred_ref, grad_ref,
    raw, joined, vec_w, vec_r, v_all, u_all, f_send, f_recv, a_send, a_recv,
    acc_p, acc_g, own_sum, part_send, part_recv, ranks, present,
    raw_sem, rank_sem, own_sem, x_send, x_recv, v_ssem, v_rsem, u_ssem, u_rsem,
    f_ssem, f_rsem, a_ssem, a_rsem, p_ssem, p_rsem, stage_sem,
):
    t = lax.axis_index("tile")
    p = lax.axis_index("panel")
    me = t // PANELS
    low = t % PANELS
    q = (p + PANELS - low) % PANELS
    alone = q == low

    row, col = me // SIDE, me % SIDE

    def place(spot):
        return (row + spot[0]) % SIDE, (col + spot[1]) % SIDE

    def slot(spot):
        y, z = place(spot)
        return SIDE * y + z

    def view(ref, chunk, *rest):
        y, z = place(chunk[0])
        return ref.at[(y if len(chunk) == 1 else slice(None), z) + rest]

    def device_at(y, z, kind):
        return {"tile": PANELS * (SIDE * y + z) + kind, "panel": p}

    left, above = device_at(0, me - 1, low), device_at(0, me - SIDE, low)
    right, below = device_at(0, me + 1, low), device_at(0, me + SIDE, low)
    has_right = col < SIDE - 1
    has_below = jnp.logical_and(col == 0, row < SIDE - 1)
    mirror = device_at(row, col, q)

    def signal(sem, device):
        pl.semaphore_signal(sem, inc=1, device_id=(device["tile"], device["panel"]), device_id_type=MESH)

    raw_copies = [
        pltpu.make_async_copy(wave_hbm, raw.at[0], raw_sem.at[0]),
        pltpu.make_async_copy(resid_hbm, raw.at[1], raw_sem.at[1]),
    ]
    rank_copies = [
        pltpu.make_async_copy(rank_hbm, ranks, rank_sem.at[0]),
        pltpu.make_async_copy(present_hbm, present, rank_sem.at[1]),
    ]
    own_copies = [
        pltpu.make_async_copy(v_hbm.at[:, :, q], v_all.at[:, :, :, p], own_sem.at[0]),
        pltpu.make_async_copy(u_hbm.at[:, :, q], u_all.at[:, :, :, p], own_sem.at[1]),
    ]
    for copy in raw_copies + rank_copies:
        copy.start()

    barrier = pltpu.get_barrier_semaphore()
    for d in (1, 2, 3):
        pl.semaphore_signal(barrier, inc=1, device_id=(t, (p + d) % PANELS), device_id_type=MESH)

    @pl.when(jnp.logical_not(alone))
    def _():
        signal(barrier, mirror)

    def tell_children(sem):
        @pl.when(has_right)
        def _():
            signal(sem, right)

        @pl.when(has_below)
        def _():
            signal(sem, below)

    tell_children(barrier)
    for copy in own_copies:
        copy.start()
    for copy in raw_copies:
        copy.wait()
    for k in (0, 1):
        joined[k, p] = jnp.concatenate([raw[k, 0], raw[k, 1]], axis=1)

    pl.semaphore_wait(barrier, 3 + (me > 0).astype(jnp.int32) + (q != low).astype(jnp.int32))

    def vec_copy(d):
        return pltpu.make_async_remote_copy(
            joined.at[:, p], joined.at[:, p], x_send.at[d - 1], x_recv.at[d - 1],
            device_id=(t, (p + d) % PANELS), device_id_type=MESH,
        )

    def vec_arrival(d):
        source = (p + PANELS - d) % PANELS
        return pltpu.make_async_remote_copy(
            joined.at[:, source], joined.at[:, source], x_send.at[d - 1], x_recv.at[d - 1],
            device_id=(t, source), device_id_type=MESH,
        )

    def factor_copy(src, dst, ssem, rsem, c, chunk, d):
        return pltpu.make_async_remote_copy(
            view(src, chunk, (q + d) % PANELS),
            view(dst, chunk, slice(None), p),
            ssem.at[c, d - 1], rsem.at[c, d - 1],
            device_id=(t, (p + d) % PANELS), device_id_type=MESH,
        )

    def factor_arrival(src, dst, ssem, rsem, c, chunk, d):
        source = (p + PANELS - d) % PANELS
        return pltpu.make_async_remote_copy(
            view(src, chunk, q),
            view(dst, chunk, slice(None), source),
            ssem.at[c, d - 1], rsem.at[c, d - 1],
            device_id=(t, source), device_id_type=MESH,
        )

    for d in (1, 3, 2):
        vec_copy(d).start()
    v_parts = (v_hbm, v_all, v_ssem, v_rsem)
    u_parts = (u_hbm, u_all, u_ssem, u_rsem)
    plan = [(v_parts, c, chunk) for c, chunk in enumerate(V_CHUNKS)]
    plan += [(u_parts, c, chunk) for c, chunk in enumerate(U_CHUNKS)]
    started = []

    def send_until(last):
        for parts, c, chunk in plan[len(started) : last]:
            started.append(c)
            for d in (2, 1, 3):
                factor_copy(*parts, c, chunk, d).start()

    send_until(LOOKAHEAD)
    @pl.when(has_right)
    def _():
        pl.semaphore_wait(stage_sem.at[0], 1)

    @pl.when(has_below)
    def _():
        pl.semaphore_wait(stage_sem.at[3], 1)

    @pl.when(col > 0)
    def _():
        signal(stage_sem.at[0], left)

    @pl.when(jnp.logical_and(col == 0, row > 0))
    def _():
        signal(stage_sem.at[3], above)

    @pl.when(me > 0)
    def _():
        pl.semaphore_wait(stage_sem.at[1], 1)

    tell_children(stage_sem.at[1])

    @pl.when(jnp.logical_not(alone))
    def _():
        signal(stage_sem.at[2], mirror)
        pl.semaphore_wait(stage_sem.at[2], 1)

    acc_p[...] = jnp.zeros_like(acc_p)
    acc_g[...] = jnp.zeros_like(acc_g)
    for copy in rank_copies:
        copy.wait()
    for d in (1, 3, 2):
        vec_arrival(d).wait_recv()
    for k, vec in ((0, vec_w), (1, vec_r)):
        rows = joined[k].reshape(256, 128).astype(jnp.float32).T
        vec[:, :256] = rows.astype(jnp.bfloat16)
        vec[:, 256:] = jnp.concatenate([rows[64:], -rows[:64]], axis=0).astype(jnp.bfloat16)

    def block_copy(send, recv, ssem, rsem, n):
        return pltpu.make_async_remote_copy(
            send.at[n], recv.at[me], ssem.at[n], rsem.at[me],
            device_id=(PANELS * n + q, p), device_id_type=MESH,
        )

    def block_own(send, recv, rsem, n):
        return pltpu.make_async_copy(send.at[n], recv.at[n], rsem.at[n])

    levels = lax.broadcasted_iota(jnp.int32, (1, 128), 1)

    def project(factor, vec, send, recv, ssem, rsem, chunk, column):
        for at in range(0, len(chunk), 2):
            slots = [slot(spot) for spot in chunk[at : at + 2]]
            joint = [factor[place(spot)].reshape(512, 128) for spot in chunk[at : at + 2]]
            joint = joint[0] if len(slots) == 1 else jnp.concatenate(joint, axis=1)
            space = jnp.dot(vec[...], joint, preferred_element_type=jnp.float32)
            for k, n in enumerate(slots):
                other = PANELS * n + q
                if column:
                    rank, here = ranks[other, t], present[other, t]
                else:
                    rank, here = ranks[t, other], present[t, other]
                limit = jnp.where(here == 1, rank, 0)
                part = jnp.where(levels < limit, space[:, 128 * k : 128 * (k + 1)], 0.0)
                send[n] = part.astype(jnp.bfloat16)

                @pl.when(other != t)
                def _():
                    block_copy(send, recv, ssem, rsem, n).start()

                @pl.when(other == t)
                def _():
                    block_own(send, recv, rsem, n).start()

    def expand(factor, recv, rsem, acc, chunk):
        for at in range(0, len(chunk), 2):
            slots = [slot(spot) for spot in chunk[at : at + 2]]
            for n in slots:
                block_own(recv, recv, rsem, n).wait()
            left = [factor[place(spot)].reshape(512, 128) for spot in chunk[at : at + 2]]
            right = [recv[n] for n in slots]
            left = left[0] if len(slots) == 1 else jnp.concatenate(left, axis=1)
            right = right[0] if len(slots) == 1 else jnp.concatenate(right, axis=1)
            acc[...] += lax.dot_general(
                left, right, (((1,), (1,)), ((), ())), preferred_element_type=jnp.float32
            )

    def part_copy(k, d):
        target = (p + d) % PANELS
        return pltpu.make_async_remote_copy(
            part_send.at[k, target], part_recv.at[k, d - 1], p_ssem.at[k, d - 1], p_rsem.at[k, d - 1],
            device_id=(t, target), device_id_type=MESH,
        )

    def send_parts(k, acc):
        lanes = lax.broadcasted_iota(jnp.int32, (256, 128), 1)
        turned = pltpu.roll(acc[256:, :], 64, 1)
        total = acc[:256, :] + jnp.where(lanes < 64, -turned, turned)
        total = total.reshape(PANELS, 64, 128)
        own_sum[k] = total
        part_send[k] = total.astype(jnp.bfloat16)
        for d in (2, 1, 3):
            part_copy(k, d).start()

    def finish(k, out):
        for d in (1, 3, 2):
            part_copy(k, d).wait_recv()
        total = own_sum[k, p]
        for d in (1, 2, 3):
            total = total + part_recv[k, d - 1].astype(jnp.float32)
        out[0] = total[:, :64].astype(jnp.bfloat16)
        out[1] = total[:, 64:].astype(jnp.bfloat16)

    own_copies[0].wait()
    for c, chunk in enumerate(V_CHUNKS):
        for d in (1, 3, 2):
            factor_arrival(*v_parts, c, chunk, d).wait_recv()
        send_until(c + 1 + LOOKAHEAD)
        project(v_all, vec_w, f_send, f_recv, f_ssem, f_rsem, chunk, True)
    own_copies[1].wait()
    for c, chunk in enumerate(U_CHUNKS):
        for d in (1, 3, 2):
            factor_arrival(*u_parts, c, chunk, d).wait_recv()
        send_until(len(V_CHUNKS) + c + 1 + LOOKAHEAD)
        project(u_all, vec_r, a_send, a_recv, a_ssem, a_rsem, chunk, False)
        expand(u_all, f_recv, f_rsem, acc_p, chunk)
    send_parts(0, acc_p)
    expand(v_all, a_recv, a_rsem, acc_g, sum((opposite(chunk) for chunk in U_CHUNKS), ()))
    send_parts(1, acc_g)
    finish(0, pred_ref)
    finish(1, grad_ref)

    for d in (1, 2, 3):
        vec_copy(d).wait_send()
        for c, chunk in enumerate(V_CHUNKS):
            factor_copy(*v_parts, c, chunk, d).wait_send()
        for c, chunk in enumerate(U_CHUNKS):
            factor_copy(*u_parts, c, chunk, d).wait_send()
        for k in (0, 1):
            part_copy(k, d).wait_send()

    def settle(n, carry):
        @pl.when(PANELS * n + q != t)
        def _():
            block_copy(f_send, f_recv, f_ssem, f_rsem, n).wait_send()
            block_copy(a_send, a_recv, a_ssem, a_rsem, n).wait_send()

        return carry

    lax.fori_loop(0, groups, settle, 0)


def on_device(wavefield, residual, v_factors, u_factors, tile_ranks, tile_present):
    tiles = tile_ranks.shape[0]
    groups = tiles // PANELS
    v_local = v_factors.reshape(SIDE, SIDE, PANELS, 2, 64, 128)
    u_local = u_factors.reshape(SIDE, SIDE, PANELS, 2, 64, 128)
    hbm = pl.BlockSpec(memory_space=pl.ANY)
    vmem = pl.BlockSpec(memory_space=pltpu.VMEM)
    b16, f32 = jnp.bfloat16, jnp.float32
    dma = pltpu.SemaphoreType.DMA
    result = jax.ShapeDtypeStruct((2, 64, 64), b16)
    pred, grad = pl.pallas_call(
        functools.partial(kernel, groups),
        out_shape=(result, result),
        in_specs=[hbm] * 6,
        out_specs=(vmem, vmem),
        scratch_shapes=[
            pltpu.VMEM((2, 2, 64, 64), b16),
            pltpu.VMEM((2, PANELS, 64, 128), b16),
            pltpu.VMEM((128, 512), b16),
            pltpu.VMEM((128, 512), b16),
            pltpu.VMEM((SIDE, SIDE, 2, PANELS, 64, 128), b16),
            pltpu.VMEM((SIDE, SIDE, 2, PANELS, 64, 128), b16),
            pltpu.VMEM((groups, 128, 128), b16),
            pltpu.VMEM((groups, 128, 128), b16),
            pltpu.VMEM((groups, 128, 128), b16),
            pltpu.VMEM((groups, 128, 128), b16),
            pltpu.VMEM((512, 128), f32),
            pltpu.VMEM((512, 128), f32),
            pltpu.VMEM((2, PANELS, 64, 128), f32),
            pltpu.VMEM((2, PANELS, 64, 128), b16),
            pltpu.VMEM((2, 3, 64, 128), b16),
            pltpu.SMEM((tiles, tiles), jnp.int32),
            pltpu.SMEM((tiles, tiles), jnp.int32),
            dma((2,)), dma((2,)), dma((2,)),
            dma((3,)), dma((3,)),
            dma((len(V_CHUNKS), 3)), dma((len(V_CHUNKS), 3)),
            dma((len(U_CHUNKS), 3)), dma((len(U_CHUNKS), 3)),
            dma((groups,)), dma((groups,)), dma((groups,)), dma((groups,)),
            dma((2, 3)), dma((2, 3)),
            pltpu.SemaphoreType.REGULAR((4,)),
        ],
        compiler_params=pltpu.CompilerParams(
            collective_id=0, has_side_effects=True, vmem_limit_bytes=60 << 20
        ),
        cost_estimate=pl.CostEstimate(flops=1 << 30, bytes_accessed=4 << 20, transcendentals=0),
    )(wavefield, residual, v_local, u_local, tile_ranks, tile_present)
    return pred, grad


def solution(mesh):
    return jax.shard_map(
        on_device,
        mesh=mesh,
        in_specs=(
            P(None, ("tile", "panel"), None),
            P(None, ("tile", "panel"), None),
            P(None, "tile", None, "panel", None),
            P("tile", None, None, "panel", None),
            P(),
            P(),
        ),
        out_specs=(P(None, ("tile", "panel"), None), P(None, ("tile", "panel"), None)),
        check_vma=False,
    )
```

```python
import functools

import jax
import jax.numpy as jnp
from jax import lax
from jax.experimental import pallas as pl
from jax.experimental.pallas import tpu as pltpu
from jax.sharding import PartitionSpec as P

MESH = pl.DeviceIdType.MESH
PANELS = 4
SIDE = 4
FAR_FIRST = (2, 1, 3, 0)
LOOKAHEAD = 4


def column(z):
    return tuple((y, z) for y in FAR_FIRST)


V_CHUNKS = tuple(column(z) for z in FAR_FIRST)
U_CHUNKS = (
    column(2),
    ((2, 1), (2, 3), (1, 1), (3, 3)),
    ((3, 1), (1, 3), (0, 1), (0, 3)),
    ((2, 0),),
    ((1, 0),),
    ((3, 0),),
    ((0, 0),),
)
ADJOINT_AFTER = {}


def pieces(chunk):
    if len(chunk) == SIDE and len({z for _, z in chunk}) == 1:
        return (chunk,)
    return tuple((spot,) for spot in chunk)


def numbered(chunks):
    count = 0
    result = []
    for chunk in chunks:
        parts = pieces(chunk)
        result.append((chunk, tuple((count + k, part) for k, part in enumerate(parts))))
        count += len(parts)
    return tuple(result), count


V_PLAN, V_COUNT = numbered(V_CHUNKS)
U_PLAN, U_COUNT = numbered(U_CHUNKS)


def opposite(chunk):
    return tuple(((SIDE - y) % SIDE, (SIDE - z) % SIDE) for y, z in chunk)


def kernel(
    groups,
    wave_hbm, resid_hbm, v_hbm, u_hbm, rank_hbm, present_hbm,
    out_ref,
    raw, joined, vec_w, vec_r, v_all, u_all, f_send, f_recv, a_send, a_recv,
    acc_p, acc_g, own_sum, part_send, part_recv, ranks, present,
    raw_sem, rank_sem, own_sem, x_send, x_recv, v_ssem, v_rsem, u_ssem, u_rsem,
    f_ssem, f_rsem, a_ssem, a_rsem, p_ssem, p_rsem, stage_sem,
):
    t = lax.axis_index("tile")
    p = lax.axis_index("panel")
    me = t // PANELS
    low = t % PANELS
    q = (p + PANELS - low) % PANELS
    alone = q == low

    row, col = me // SIDE, me % SIDE

    def place(spot):
        return (row + spot[0]) % SIDE, (col + spot[1]) % SIDE

    def slot(spot):
        y, z = place(spot)
        return SIDE * y + z

    def view(ref, chunk, *rest):
        y, z = place(chunk[0])
        return ref.at[(y if len(chunk) == 1 else slice(None), z) + rest]

    def device_at(y, z, kind):
        return {"tile": PANELS * (SIDE * y + z) + kind, "panel": p}

    left, above = device_at(0, me - 1, low), device_at(0, me - SIDE, low)
    right, below = device_at(0, me + 1, low), device_at(0, me + SIDE, low)
    has_right = col < SIDE - 1
    has_below = jnp.logical_and(col == 0, row < SIDE - 1)
    mirror = device_at(row, col, q)

    def signal(sem, device):
        pl.semaphore_signal(sem, inc=1, device_id=(device["tile"], device["panel"]), device_id_type=MESH)

    raw_copies = [
        pltpu.make_async_copy(wave_hbm, raw.at[0], raw_sem.at[0]),
        pltpu.make_async_copy(resid_hbm, raw.at[1], raw_sem.at[1]),
    ]
    rank_copies = [
        pltpu.make_async_copy(rank_hbm, ranks, rank_sem.at[0]),
        pltpu.make_async_copy(present_hbm, present, rank_sem.at[1]),
    ]
    own_copies = [
        pltpu.make_async_copy(v_hbm.at[:, :, q], v_all.at[:, :, :, p], own_sem.at[0]),
        pltpu.make_async_copy(u_hbm.at[:, :, q], u_all.at[:, :, :, p], own_sem.at[1]),
    ]
    for copy in raw_copies + rank_copies:
        copy.start()

    barrier = pltpu.get_barrier_semaphore()
    for d in (1, 2, 3):
        pl.semaphore_signal(barrier, inc=1, device_id=(t, (p + d) % PANELS), device_id_type=MESH)

    @pl.when(jnp.logical_not(alone))
    def _():
        signal(barrier, mirror)

    def tell_children(sem):
        @pl.when(has_right)
        def _():
            signal(sem, right)

        @pl.when(has_below)
        def _():
            signal(sem, below)

    tell_children(barrier)
    for copy in own_copies:
        copy.start()
    pl.semaphore_wait(barrier, 3 + (me > 0).astype(jnp.int32) + (q != low).astype(jnp.int32))

    def vec_copy(d):
        return pltpu.make_async_remote_copy(
            joined.at[:, p], joined.at[:, p], x_send.at[d - 1], x_recv.at[d - 1],
            device_id=(t, (p + d) % PANELS), device_id_type=MESH,
        )

    def vec_arrival(d):
        source = (p + PANELS - d) % PANELS
        return pltpu.make_async_remote_copy(
            joined.at[:, source], joined.at[:, source], x_send.at[d - 1], x_recv.at[d - 1],
            device_id=(t, source), device_id_type=MESH,
        )

    def factor_copy(src, dst, ssem, rsem, c, chunk, d):
        return pltpu.make_async_remote_copy(
            view(src, chunk, (q + d) % PANELS),
            view(dst, chunk, slice(None), p),
            ssem.at[c, d - 1], rsem.at[c, d - 1],
            device_id=(t, (p + d) % PANELS), device_id_type=MESH,
        )

    def factor_arrival(src, dst, ssem, rsem, c, chunk, d):
        source = (p + PANELS - d) % PANELS
        return pltpu.make_async_remote_copy(
            view(src, chunk, q),
            view(dst, chunk, slice(None), source),
            ssem.at[c, d - 1], rsem.at[c, d - 1],
            device_id=(t, source), device_id_type=MESH,
        )

    v_parts = (v_hbm, v_all, v_ssem, v_rsem)
    u_parts = (u_hbm, u_all, u_ssem, u_rsem)
    plan = [(v_parts, parts) for _, parts in V_PLAN] + [(u_parts, parts) for _, parts in U_PLAN]
    started = []

    def send_until(last):
        for refs, parts in plan[len(started) : last]:
            started.append(refs)
            for c, part in parts:
                for d in (2, 1, 3):
                    factor_copy(*refs, c, part, d).start()

    send_until(1)
    for copy in raw_copies:
        copy.wait()
    for k in (0, 1):
        joined[k, p] = jnp.concatenate([raw[k, 0], raw[k, 1]], axis=1)
    for d in (2, 1, 3):
        vec_copy(d).start()
    send_until(LOOKAHEAD)
    @pl.when(has_right)
    def _():
        pl.semaphore_wait(stage_sem.at[0], 1)

    @pl.when(has_below)
    def _():
        pl.semaphore_wait(stage_sem.at[3], 1)

    @pl.when(col > 0)
    def _():
        signal(stage_sem.at[0], left)

    @pl.when(jnp.logical_and(col == 0, row > 0))
    def _():
        signal(stage_sem.at[3], above)

    @pl.when(me > 0)
    def _():
        pl.semaphore_wait(stage_sem.at[1], 1)

    @pl.when(me == 0)
    def _():
        def answer(n, carry):
            signal(stage_sem.at[1], device_at(0, n, low))
            return carry

        lax.fori_loop(1, groups, answer, 0)

    @pl.when(jnp.logical_not(alone))
    def _():
        signal(stage_sem.at[2], mirror)
        pl.semaphore_wait(stage_sem.at[2], 1)

    acc_p[...] = jnp.zeros_like(acc_p)
    acc_g[...] = jnp.zeros_like(acc_g)
    for copy in rank_copies:
        copy.wait()
    for d in (1, 3, 2):
        vec_arrival(d).wait_recv()
    for k, vec in ((0, vec_w), (1, vec_r)):
        rows = joined[k].reshape(256, 128).astype(jnp.float32).T
        vec[:, :256] = rows.astype(jnp.bfloat16)
        vec[:, 256:] = jnp.concatenate([rows[64:], -rows[:64]], axis=0).astype(jnp.bfloat16)

    def block_copy(send, recv, ssem, rsem, n):
        return pltpu.make_async_remote_copy(
            send.at[n], recv.at[me], ssem.at[n], rsem.at[me],
            device_id=(PANELS * n + q, p), device_id_type=MESH,
        )

    def block_own(send, recv, rsem, n):
        return pltpu.make_async_copy(send.at[n], recv.at[n], rsem.at[n])

    levels = lax.broadcasted_iota(jnp.int32, (1, 128), 1)

    def project(factor, vec, send, recv, ssem, rsem, chunk, column):
        for at in range(0, len(chunk), 2):
            slots = [slot(spot) for spot in chunk[at : at + 2]]
            joint = [factor[place(spot)].reshape(512, 128) for spot in chunk[at : at + 2]]
            joint = joint[0] if len(slots) == 1 else jnp.concatenate(joint, axis=1)
            space = jnp.dot(vec[...], joint, preferred_element_type=jnp.float32)
            for k, n in enumerate(slots):
                other = PANELS * n + q
                if column:
                    rank, here = ranks[other, t], present[other, t]
                else:
                    rank, here = ranks[t, other], present[t, other]
                limit = jnp.where(here == 1, rank, 0)
                part = jnp.where(levels < limit, space[:, 128 * k : 128 * (k + 1)], 0.0)
                send[n] = part.astype(jnp.bfloat16)

                @pl.when(other != t)
                def _():
                    block_copy(send, recv, ssem, rsem, n).start()

                @pl.when(other == t)
                def _():
                    block_own(send, recv, rsem, n).start()

    def expand(factor, recv, rsem, acc, chunk):
        for at in range(0, len(chunk), 2):
            slots = [slot(spot) for spot in chunk[at : at + 2]]
            for n in slots:
                block_own(recv, recv, rsem, n).wait()
            left = [factor[place(spot)].reshape(512, 128) for spot in chunk[at : at + 2]]
            right = [recv[n] for n in slots]
            left = left[0] if len(slots) == 1 else jnp.concatenate(left, axis=1)
            right = right[0] if len(slots) == 1 else jnp.concatenate(right, axis=1)
            acc[...] += lax.dot_general(
                left, right, (((1,), (1,)), ((), ())), preferred_element_type=jnp.float32
            )

    def part_copy(k, d):
        target = (p + d) % PANELS
        return pltpu.make_async_remote_copy(
            part_send.at[k, target], part_recv.at[k, d - 1], p_ssem.at[k, d - 1], p_rsem.at[k, d - 1],
            device_id=(t, target), device_id_type=MESH,
        )

    def send_parts(k, acc):
        lanes = lax.broadcasted_iota(jnp.int32, (256, 128), 1)
        turned = pltpu.roll(acc[256:, :], 64, 1)
        total = acc[:256, :] + jnp.where(lanes < 64, -turned, turned)
        total = total.reshape(PANELS, 64, 128)
        own_sum[k] = total
        part_send[k] = total.astype(jnp.bfloat16)
        for d in (2, 1, 3):
            part_copy(k, d).start()

    def finish(k):
        for d in (1, 3, 2):
            part_copy(k, d).wait_recv()
        total = own_sum[k, p]
        for d in (1, 2, 3):
            total = total + part_recv[k, d - 1].astype(jnp.float32)
        out_ref[k, 0] = total[:, :64].astype(jnp.bfloat16)
        out_ref[k, 1] = total[:, 64:].astype(jnp.bfloat16)

    def arrive(refs, parts):
        for c, part in parts:
            for d in (1, 3, 2):
                factor_arrival(*refs, c, part, d).wait_recv()

    own_copies[0].wait()
    for c, (chunk, parts) in enumerate(V_PLAN):
        arrive(v_parts, parts)
        send_until(c + 1 + LOOKAHEAD)
        project(v_all, vec_w, f_send, f_recv, f_ssem, f_rsem, chunk, True)
    own_copies[1].wait()
    done = []
    for c, (chunk, parts) in enumerate(U_PLAN):
        arrive(u_parts, parts)
        send_until(len(V_PLAN) + c + 1 + LOOKAHEAD)
        project(u_all, vec_r, a_send, a_recv, a_ssem, a_rsem, chunk, False)
        expand(u_all, f_recv, f_rsem, acc_p, chunk)
        for k in ADJOINT_AFTER.get(c, ()):
            expand(v_all, a_recv, a_rsem, acc_g, opposite(U_CHUNKS[k]))
            done.append(k)
    send_parts(0, acc_p)
    rest = sum((opposite(chunk) for k, chunk in enumerate(U_CHUNKS) if k not in done), ())
    expand(v_all, a_recv, a_rsem, acc_g, rest)
    send_parts(1, acc_g)

    for d in (1, 2, 3):
        vec_copy(d).wait_send()
        for refs, parts in plan:
            for c, part in parts:
                factor_copy(*refs, c, part, d).wait_send()

    def settle(n, carry):
        @pl.when(PANELS * n + q != t)
        def _():
            block_copy(f_send, f_recv, f_ssem, f_rsem, n).wait_send()
            block_copy(a_send, a_recv, a_ssem, a_rsem, n).wait_send()

        return carry

    lax.fori_loop(0, groups, settle, 0)
    finish(0)
    finish(1)
    for d in (1, 2, 3):
        for k in (0, 1):
            part_copy(k, d).wait_send()


def on_device(wavefield, residual, v_factors, u_factors, tile_ranks, tile_present):
    tiles = tile_ranks.shape[0]
    groups = tiles // PANELS
    v_local = v_factors.reshape(SIDE, SIDE, PANELS, 2, 64, 128)
    u_local = u_factors.reshape(SIDE, SIDE, PANELS, 2, 64, 128)
    hbm = pl.BlockSpec(memory_space=pl.ANY)
    vmem = pl.BlockSpec(memory_space=pltpu.VMEM)
    b16, f32 = jnp.bfloat16, jnp.float32
    dma = pltpu.SemaphoreType.DMA
    packed = pl.pallas_call(
        functools.partial(kernel, groups),
        out_shape=jax.ShapeDtypeStruct((2, 2, 64, 64), b16),
        in_specs=[hbm] * 6,
        out_specs=vmem,
        scratch_shapes=[
            pltpu.VMEM((2, 2, 64, 64), b16),
            pltpu.VMEM((2, PANELS, 64, 128), b16),
            pltpu.VMEM((128, 512), b16),
            pltpu.VMEM((128, 512), b16),
            pltpu.VMEM((SIDE, SIDE, 2, PANELS, 64, 128), b16),
            pltpu.VMEM((SIDE, SIDE, 2, PANELS, 64, 128), b16),
            pltpu.VMEM((groups, 128, 128), b16),
            pltpu.VMEM((groups, 128, 128), b16),
            pltpu.VMEM((groups, 128, 128), b16),
            pltpu.VMEM((groups, 128, 128), b16),
            pltpu.VMEM((512, 128), f32),
            pltpu.VMEM((512, 128), f32),
            pltpu.VMEM((2, PANELS, 64, 128), f32),
            pltpu.VMEM((2, PANELS, 64, 128), b16),
            pltpu.VMEM((2, 3, 64, 128), b16),
            pltpu.SMEM((tiles, tiles), jnp.int32),
            pltpu.SMEM((tiles, tiles), jnp.int32),
            dma((2,)), dma((2,)), dma((2,)),
            dma((3,)), dma((3,)),
            dma((V_COUNT, 3)), dma((V_COUNT, 3)),
            dma((U_COUNT, 3)), dma((U_COUNT, 3)),
            dma((groups,)), dma((groups,)), dma((groups,)), dma((groups,)),
            dma((2, 3)), dma((2, 3)),
            pltpu.SemaphoreType.REGULAR((4,)),
        ],
        compiler_params=pltpu.CompilerParams(
            collective_id=0, has_side_effects=True, vmem_limit_bytes=32 << 20
        ),
        cost_estimate=pl.CostEstimate(flops=1 << 30, bytes_accessed=4 << 20, transcendentals=0),
    )(*[pltpu.with_memory_space_constraint(x, pltpu.HBM) for x in (wavefield, residual, v_local, u_local, tile_ranks, tile_present)])
    return packed[0], packed[1]


def solution(mesh):
    return jax.shard_map(
        on_device,
        mesh=mesh,
        in_specs=(
            P(None, ("tile", "panel"), None),
            P(None, ("tile", "panel"), None),
            P(None, "tile", None, "panel", None),
            P("tile", None, None, "panel", None),
            P(),
            P(),
        ),
        out_specs=(P(None, ("tile", "panel"), None), P(None, ("tile", "panel"), None)),
        check_vma=False,
    )
```

```python
import functools

import jax
import jax.numpy as jnp
from jax import lax
from jax.experimental import pallas as pl
from jax.experimental.pallas import tpu as pltpu
from jax.sharding import PartitionSpec as P

MESH = pl.DeviceIdType.MESH
PANELS = 4
SIDE = 4
FAR_FIRST = (2, 1, 3, 0)
LOOKAHEAD = 6


def column(z):
    return tuple((y, z) for y in FAR_FIRST)


FAR_CHUNKS = (
    column(2),
    ((2, 1), (2, 3), (1, 1), (3, 3)),
    ((3, 1), (1, 3), (0, 1), (0, 3)),
)
V_CHUNKS = FAR_CHUNKS + (column(0),)
U_CHUNKS = FAR_CHUNKS + tuple((spot,) for spot in column(0))
ORDER = ("v", "v", "v", "u", "u", "u", "v", "u", "u", "u", "u")


def pieces(chunk):
    if len(chunk) == SIDE and len({z for _, z in chunk}) == 1:
        return (chunk,)
    return tuple((spot,) for spot in chunk)


def numbered(chunks):
    count = 0
    result = []
    for chunk in chunks:
        parts = pieces(chunk)
        result.append((chunk, tuple((count + k, part) for k, part in enumerate(parts))))
        count += len(parts)
    return tuple(result), count


V_PLAN, V_COUNT = numbered(V_CHUNKS)
U_PLAN, U_COUNT = numbered(U_CHUNKS)


def opposite(chunk):
    return tuple(((SIDE - y) % SIDE, (SIDE - z) % SIDE) for y, z in chunk)


def kernel(
    groups,
    wave_hbm, resid_hbm, v_hbm, u_hbm, rank_hbm, present_hbm,
    out_ref,
    raw, joined, vec_w, vec_r, v_all, u_all, f_send, f_recv, a_send, a_recv,
    acc_p, acc_g, own_sum, part_send, part_recv, ranks, present,
    raw_sem, rank_sem, own_sem, x_send, x_recv, v_ssem, v_rsem, u_ssem, u_rsem,
    f_ssem, f_rsem, a_ssem, a_rsem, p_ssem, p_rsem, stage_sem,
):
    t = lax.axis_index("tile")
    p = lax.axis_index("panel")
    me = t // PANELS
    low = t % PANELS
    q = (p + PANELS - low) % PANELS
    mine = low // 2 * 2 + 1 - low % 2
    theirs = q // 2 * 2 + 1 - q % 2

    row, col = me // SIDE, me % SIDE

    def place(spot):
        return (row + spot[0]) % SIDE, (col + spot[1]) % SIDE

    def slot(spot):
        y, z = place(spot)
        return SIDE * y + z

    def view(ref, chunk, *rest):
        y, z = place(chunk[0])
        return ref.at[(y if len(chunk) == 1 else slice(None), z) + rest]

    def device_at(y, z, kind):
        return {"tile": PANELS * (SIDE * y + z) + kind, "panel": p}

    left, above = device_at(0, me - 1, low), device_at(0, me - SIDE, low)
    right, below = device_at(0, me + 1, low), device_at(0, me + SIDE, low)
    has_right = col < SIDE - 1
    has_below = jnp.logical_and(col == 0, row < SIDE - 1)
    mirror = device_at(row, col, q)

    def signal(sem, device):
        pl.semaphore_signal(sem, inc=1, device_id=(device["tile"], device["panel"]), device_id_type=MESH)

    raw_copies = [
        pltpu.make_async_copy(wave_hbm, raw.at[0], raw_sem.at[0]),
        pltpu.make_async_copy(resid_hbm, raw.at[1], raw_sem.at[1]),
    ]
    rank_copies = [
        pltpu.make_async_copy(rank_hbm, ranks, rank_sem.at[0]),
        pltpu.make_async_copy(present_hbm, present, rank_sem.at[1]),
    ]
    own_copies = [
        pltpu.make_async_copy(v_hbm.at[:, :, q], v_all.at[:, :, :, p], own_sem.at[0]),
        pltpu.make_async_copy(u_hbm.at[:, :, q], u_all.at[:, :, :, p], own_sem.at[1]),
    ]

    barrier = pltpu.get_barrier_semaphore()
    for d in (1, 2, 3):
        pl.semaphore_signal(barrier, inc=1, device_id=(t, (p + d) % PANELS), device_id_type=MESH)

    @pl.when(mine < theirs)
    def _():
        signal(barrier, mirror)

    def tell_children(sem):
        @pl.when(has_right)
        def _():
            signal(sem, right)

        @pl.when(has_below)
        def _():
            signal(sem, below)

    tell_children(barrier)
    for copy in raw_copies + rank_copies + own_copies:
        copy.start()
    pl.semaphore_wait(barrier, 3 + (me > 0).astype(jnp.int32) + (theirs < mine).astype(jnp.int32))

    def vec_copy(d):
        return pltpu.make_async_remote_copy(
            joined.at[:, p], joined.at[:, p], x_send.at[d - 1], x_recv.at[d - 1],
            device_id=(t, (p + d) % PANELS), device_id_type=MESH,
        )

    def vec_arrival(d):
        source = (p + PANELS - d) % PANELS
        return pltpu.make_async_remote_copy(
            joined.at[:, source], joined.at[:, source], x_send.at[d - 1], x_recv.at[d - 1],
            device_id=(t, source), device_id_type=MESH,
        )

    def factor_copy(src, dst, ssem, rsem, c, chunk, d):
        return pltpu.make_async_remote_copy(
            view(src, chunk, (q + d) % PANELS),
            view(dst, chunk, slice(None), p),
            ssem.at[c, d - 1], rsem.at[c, d - 1],
            device_id=(t, (p + d) % PANELS), device_id_type=MESH,
        )

    def factor_arrival(src, dst, ssem, rsem, c, chunk, d):
        source = (p + PANELS - d) % PANELS
        return pltpu.make_async_remote_copy(
            view(src, chunk, q),
            view(dst, chunk, slice(None), source),
            ssem.at[c, d - 1], rsem.at[c, d - 1],
            device_id=(t, source), device_id_type=MESH,
        )

    v_parts = (v_hbm, v_all, v_ssem, v_rsem)
    u_parts = (u_hbm, u_all, u_ssem, u_rsem)
    left_to_plan = {"v": list(V_PLAN), "u": list(U_PLAN)}
    steps = [(kind,) + left_to_plan[kind].pop(0) for kind in ORDER]
    plan = [(v_parts if kind == "v" else u_parts, parts) for kind, _, parts in steps]
    started = []

    def send_until(last):
        for refs, parts in plan[len(started) : last]:
            started.append(refs)
            for c, part in parts:
                for d in (2, 1, 3):
                    factor_copy(*refs, c, part, d).start()

    send_until(1)
    for copy in raw_copies:
        copy.wait()
    for k in (0, 1):
        joined[k, p] = jnp.concatenate([raw[k, 0], raw[k, 1]], axis=1)
    for d in (2, 1, 3):
        vec_copy(d).start()
    send_until(LOOKAHEAD)
    @pl.when(has_right)
    def _():
        pl.semaphore_wait(stage_sem.at[0], 1)

    @pl.when(has_below)
    def _():
        pl.semaphore_wait(stage_sem.at[3], 1)

    @pl.when(col > 0)
    def _():
        signal(stage_sem.at[0], left)

    @pl.when(jnp.logical_and(col == 0, row > 0))
    def _():
        signal(stage_sem.at[3], above)

    @pl.when(me > 0)
    def _():
        pl.semaphore_wait(stage_sem.at[1], 1)

    @pl.when(me == 0)
    def _():
        def answer(n, carry):
            signal(stage_sem.at[1], device_at(0, n, low))
            return carry

        lax.fori_loop(1, groups, answer, 0)

    @pl.when(theirs < mine)
    def _():
        signal(stage_sem.at[2], mirror)
        pl.semaphore_wait(stage_sem.at[2], 1)

    @pl.when(mine < theirs)
    def _():
        pl.semaphore_wait(stage_sem.at[2], 1)
        signal(stage_sem.at[2], mirror)

    acc_p[...] = jnp.zeros_like(acc_p)
    acc_g[...] = jnp.zeros_like(acc_g)
    for copy in rank_copies:
        copy.wait()
    for d in (1, 3, 2):
        vec_arrival(d).wait_recv()
    for k, vec in ((0, vec_w), (1, vec_r)):
        rows = joined[k].reshape(256, 128).astype(jnp.float32).T
        vec[:, :256] = rows.astype(jnp.bfloat16)
        vec[:, 256:] = jnp.concatenate([rows[64:], -rows[:64]], axis=0).astype(jnp.bfloat16)

    def block_copy(send, recv, ssem, rsem, n):
        return pltpu.make_async_remote_copy(
            send.at[n], recv.at[me], ssem.at[n], rsem.at[me],
            device_id=(PANELS * n + q, p), device_id_type=MESH,
        )

    def block_own(send, recv, rsem, n):
        return pltpu.make_async_copy(send.at[n], recv.at[n], rsem.at[n])

    levels = lax.broadcasted_iota(jnp.int32, (1, 128), 1)

    def project(factor, vec, send, recv, ssem, rsem, chunk, column):
        for at in range(0, len(chunk), 2):
            slots = [slot(spot) for spot in chunk[at : at + 2]]
            joint = [factor[place(spot)].reshape(512, 128) for spot in chunk[at : at + 2]]
            joint = joint[0] if len(slots) == 1 else jnp.concatenate(joint, axis=1)
            space = jnp.dot(vec[...], joint, preferred_element_type=jnp.float32)
            for k, n in enumerate(slots):
                other = PANELS * n + q
                if column:
                    rank, here = ranks[other, t], present[other, t]
                else:
                    rank, here = ranks[t, other], present[t, other]
                limit = jnp.where(here == 1, rank, 0)
                part = jnp.where(levels < limit, space[:, 128 * k : 128 * (k + 1)], 0.0)
                send[n] = part.astype(jnp.bfloat16)

                @pl.when(other != t)
                def _():
                    block_copy(send, recv, ssem, rsem, n).start()

                @pl.when(other == t)
                def _():
                    block_own(send, recv, rsem, n).start()

    def expand(factor, recv, rsem, acc, chunk):
        for at in range(0, len(chunk), 2):
            slots = [slot(spot) for spot in chunk[at : at + 2]]
            for n in slots:
                block_own(recv, recv, rsem, n).wait()
            left = [factor[place(spot)].reshape(512, 128) for spot in chunk[at : at + 2]]
            right = [recv[n] for n in slots]
            left = left[0] if len(slots) == 1 else jnp.concatenate(left, axis=1)
            right = right[0] if len(slots) == 1 else jnp.concatenate(right, axis=1)
            acc[...] += lax.dot_general(
                left, right, (((1,), (1,)), ((), ())), preferred_element_type=jnp.float32
            )

    def part_copy(k, d):
        target = (p + d) % PANELS
        return pltpu.make_async_remote_copy(
            part_send.at[k, target], part_recv.at[k, d - 1], p_ssem.at[k, d - 1], p_rsem.at[k, d - 1],
            device_id=(t, target), device_id_type=MESH,
        )

    def send_parts(k, acc):
        lanes = lax.broadcasted_iota(jnp.int32, (256, 128), 1)
        turned = pltpu.roll(acc[256:, :], 64, 1)
        total = acc[:256, :] + jnp.where(lanes < 64, -turned, turned)
        total = total.reshape(PANELS, 64, 128)
        own_sum[k] = total
        part_send[k] = total.astype(jnp.bfloat16)
        for d in (2, 1, 3):
            part_copy(k, d).start()

    def finish(k):
        for d in (1, 3, 2):
            part_copy(k, d).wait_recv()
        total = own_sum[k, p]
        for d in (1, 2, 3):
            total = total + part_recv[k, d - 1].astype(jnp.float32)
        out_ref[k, 0] = total[:, :64].astype(jnp.bfloat16)
        out_ref[k, 1] = total[:, 64:].astype(jnp.bfloat16)

    def arrive(refs, parts):
        for c, part in parts:
            for d in (1, 3, 2):
                factor_arrival(*refs, c, part, d).wait_recv()

    for copy in own_copies:
        copy.wait()
    for c, (kind, chunk, parts) in enumerate(steps):
        arrive(plan[c][0], parts)
        send_until(c + 1 + LOOKAHEAD)
        if kind == "v":
            project(v_all, vec_w, f_send, f_recv, f_ssem, f_rsem, chunk, True)
        else:
            project(u_all, vec_r, a_send, a_recv, a_ssem, a_rsem, chunk, False)
            if len(chunk) > 1:
                expand(u_all, f_recv, f_rsem, acc_p, chunk)
    expand(u_all, f_recv, f_rsem, acc_p, V_CHUNKS[-1])
    send_parts(0, acc_p)
    expand(v_all, a_recv, a_rsem, acc_g, sum((opposite(chunk) for chunk in U_CHUNKS), ()))
    send_parts(1, acc_g)

    for d in (1, 2, 3):
        vec_copy(d).wait_send()
        for refs, parts in plan:
            for c, part in parts:
                factor_copy(*refs, c, part, d).wait_send()

    def settle(n, carry):
        @pl.when(PANELS * n + q != t)
        def _():
            block_copy(f_send, f_recv, f_ssem, f_rsem, n).wait_send()
            block_copy(a_send, a_recv, a_ssem, a_rsem, n).wait_send()

        return carry

    lax.fori_loop(0, groups, settle, 0)
    finish(0)
    finish(1)
    for d in (1, 2, 3):
        for k in (0, 1):
            part_copy(k, d).wait_send()


def on_device(wavefield, residual, v_factors, u_factors, tile_ranks, tile_present):
    tiles = tile_ranks.shape[0]
    groups = tiles // PANELS
    v_local = v_factors.reshape(SIDE, SIDE, PANELS, 2, 64, 128)
    u_local = u_factors.reshape(SIDE, SIDE, PANELS, 2, 64, 128)
    hbm = pl.BlockSpec(memory_space=pl.ANY)
    vmem = pl.BlockSpec(memory_space=pltpu.VMEM)
    b16, f32 = jnp.bfloat16, jnp.float32
    dma = pltpu.SemaphoreType.DMA
    packed = pl.pallas_call(
        functools.partial(kernel, groups),
        out_shape=jax.ShapeDtypeStruct((2, 2, 64, 64), b16),
        in_specs=[hbm] * 6,
        out_specs=vmem,
        scratch_shapes=[
            pltpu.VMEM((2, 2, 64, 64), b16),
            pltpu.VMEM((2, PANELS, 64, 128), b16),
            pltpu.VMEM((128, 512), b16),
            pltpu.VMEM((128, 512), b16),
            pltpu.VMEM((SIDE, SIDE, 2, PANELS, 64, 128), b16),
            pltpu.VMEM((SIDE, SIDE, 2, PANELS, 64, 128), b16),
            pltpu.VMEM((groups, 128, 128), b16),
            pltpu.VMEM((groups, 128, 128), b16),
            pltpu.VMEM((groups, 128, 128), b16),
            pltpu.VMEM((groups, 128, 128), b16),
            pltpu.VMEM((512, 128), f32),
            pltpu.VMEM((512, 128), f32),
            pltpu.VMEM((2, PANELS, 64, 128), f32),
            pltpu.VMEM((2, PANELS, 64, 128), b16),
            pltpu.VMEM((2, 3, 64, 128), b16),
            pltpu.SMEM((tiles, tiles), jnp.int32),
            pltpu.SMEM((tiles, tiles), jnp.int32),
            dma((2,)), dma((2,)), dma((2,)),
            dma((3,)), dma((3,)),
            dma((V_COUNT, 3)), dma((V_COUNT, 3)),
            dma((U_COUNT, 3)), dma((U_COUNT, 3)),
            dma((groups,)), dma((groups,)), dma((groups,)), dma((groups,)),
            dma((2, 3)), dma((2, 3)),
            pltpu.SemaphoreType.REGULAR((4,)),
        ],
        compiler_params=pltpu.CompilerParams(
            collective_id=0, has_side_effects=True, vmem_limit_bytes=32 << 20
        ),
        cost_estimate=pl.CostEstimate(flops=1 << 30, bytes_accessed=4 << 20, transcendentals=0),
    )(*[pltpu.with_memory_space_constraint(x, pltpu.HBM) for x in (wavefield, residual, v_local, u_local, tile_ranks, tile_present)])
    return packed[0], packed[1]


def solution(mesh):
    return jax.shard_map(
        on_device,
        mesh=mesh,
        in_specs=(
            P(None, ("tile", "panel"), None),
            P(None, ("tile", "panel"), None),
            P(None, "tile", None, "panel", None),
            P("tile", None, None, "panel", None),
            P(),
            P(),
        ),
        out_specs=(P(None, ("tile", "panel"), None), P(None, ("tile", "panel"), None)),
        check_vma=False,
    )
```

```python
import functools

import jax
import jax.numpy as jnp
from jax import lax
from jax.experimental import pallas as pl
from jax.experimental.pallas import tpu as pltpu
from jax.sharding import PartitionSpec as P

MESH = pl.DeviceIdType.MESH
PANELS = 4
SIDE = 4
FAR_FIRST = (2, 1, 3, 0)
LOOKAHEAD = 6


def column(z):
    return tuple((y, z) for y in FAR_FIRST)


FAR_CHUNKS = (
    column(2),
    ((2, 1), (2, 3), (1, 1), (3, 3)),
    ((3, 1), (1, 3), (0, 1), (0, 3)),
)
V_CHUNKS = FAR_CHUNKS + (column(0),)
U_CHUNKS = FAR_CHUNKS + tuple((spot,) for spot in column(0))
ORDER = ("v", "v", "v", "u", "u", "u", "v", "u", "u", "u", "u")


def pieces(chunk):
    if len(chunk) == SIDE and len({z for _, z in chunk}) == 1:
        return (chunk,)
    return tuple((spot,) for spot in chunk)


def numbered(chunks):
    count = 0
    result = []
    for chunk in chunks:
        parts = pieces(chunk)
        result.append((chunk, tuple((count + k, part) for k, part in enumerate(parts))))
        count += len(parts)
    return tuple(result), count


V_PLAN, V_COUNT = numbered(V_CHUNKS)
U_PLAN, U_COUNT = numbered(U_CHUNKS)


def opposite(chunk):
    return tuple(((SIDE - y) % SIDE, (SIDE - z) % SIDE) for y, z in chunk)


def kernel(
    groups,
    wave_hbm, resid_hbm, v_hbm, u_hbm, rank_hbm, present_hbm,
    out_ref,
    raw, joined, vec_w, vec_r, v_all, u_all, f_send, f_recv, a_send, a_recv,
    acc_p, acc_g, own_sum, part_send, part_recv, ranks, present,
    raw_sem, rank_sem, own_sem, x_send, x_recv, v_ssem, v_rsem, u_ssem, u_rsem,
    f_ssem, f_rsem, a_ssem, a_rsem, p_ssem, p_rsem, stage_sem,
):
    t = lax.axis_index("tile")
    p = lax.axis_index("panel")
    me = t // PANELS
    low = t % PANELS
    q = (p + PANELS - low) % PANELS
    mine = low // 2 * 2 + 1 - low % 2
    theirs = q // 2 * 2 + 1 - q % 2

    row, col = me // SIDE, me % SIDE

    def place(spot):
        return (row + spot[0]) % SIDE, (col + spot[1]) % SIDE

    def slot(spot):
        y, z = place(spot)
        return SIDE * y + z

    def view(ref, chunk, *rest):
        y, z = place(chunk[0])
        return ref.at[(y if len(chunk) == 1 else slice(None), z) + rest]

    def device_at(y, z, kind):
        return {"tile": PANELS * (SIDE * y + z) + kind, "panel": p}

    left, above = device_at(0, me - 1, low), device_at(0, me - SIDE, low)
    right, below = device_at(0, me + 1, low), device_at(0, me + SIDE, low)
    has_right = col < SIDE - 1
    has_below = jnp.logical_and(col == 0, row < SIDE - 1)
    mirror = device_at(row, col, q)

    def signal(sem, device):
        pl.semaphore_signal(sem, inc=1, device_id=(device["tile"], device["panel"]), device_id_type=MESH)

    raw_copies = [
        pltpu.make_async_copy(wave_hbm, raw.at[0], raw_sem.at[0]),
        pltpu.make_async_copy(resid_hbm, raw.at[1], raw_sem.at[1]),
    ]
    rank_copies = [
        pltpu.make_async_copy(rank_hbm, ranks, rank_sem.at[0]),
        pltpu.make_async_copy(present_hbm, present, rank_sem.at[1]),
    ]
    own_copies = [
        pltpu.make_async_copy(v_hbm.at[:, :, q], v_all.at[:, :, :, p], own_sem.at[0]),
        pltpu.make_async_copy(u_hbm.at[:, :, q], u_all.at[:, :, :, p], own_sem.at[1]),
    ]

    barrier = pltpu.get_barrier_semaphore()
    for d in (1, 2, 3):
        pl.semaphore_signal(barrier, inc=1, device_id=(t, (p + d) % PANELS), device_id_type=MESH)

    @pl.when(mine < theirs)
    def _():
        signal(barrier, mirror)

    def tell_children(sem):
        @pl.when(has_right)
        def _():
            signal(sem, right)

        @pl.when(has_below)
        def _():
            signal(sem, below)

    tell_children(barrier)
    for copy in raw_copies + rank_copies + own_copies:
        copy.start()
    pl.semaphore_wait(barrier, 3 + (me > 0).astype(jnp.int32) + (theirs < mine).astype(jnp.int32))

    def vec_copy(d):
        return pltpu.make_async_remote_copy(
            joined.at[:, p], joined.at[:, p], x_send.at[d - 1], x_recv.at[d - 1],
            device_id=(t, (p + d) % PANELS), device_id_type=MESH,
        )

    def vec_arrival(d):
        source = (p + PANELS - d) % PANELS
        return pltpu.make_async_remote_copy(
            joined.at[:, source], joined.at[:, source], x_send.at[d - 1], x_recv.at[d - 1],
            device_id=(t, source), device_id_type=MESH,
        )

    def factor_copy(src, dst, ssem, rsem, c, chunk, d):
        return pltpu.make_async_remote_copy(
            view(src, chunk, (q + d) % PANELS),
            view(dst, chunk, slice(None), p),
            ssem.at[c, d - 1], rsem.at[c, d - 1],
            device_id=(t, (p + d) % PANELS), device_id_type=MESH,
        )

    def factor_arrival(src, dst, ssem, rsem, c, chunk, d):
        source = (p + PANELS - d) % PANELS
        return pltpu.make_async_remote_copy(
            view(src, chunk, q),
            view(dst, chunk, slice(None), source),
            ssem.at[c, d - 1], rsem.at[c, d - 1],
            device_id=(t, source), device_id_type=MESH,
        )

    v_parts = (v_hbm, v_all, v_ssem, v_rsem)
    u_parts = (u_hbm, u_all, u_ssem, u_rsem)
    left_to_plan = {"v": list(V_PLAN), "u": list(U_PLAN)}
    steps = [(kind,) + left_to_plan[kind].pop(0) for kind in ORDER]
    plan = [(v_parts if kind == "v" else u_parts, parts) for kind, _, parts in steps]
    started = []

    def send_until(last):
        for refs, parts in plan[len(started) : last]:
            started.append(refs)
            for c, part in parts:
                for d in (1, 3, 2):
                    factor_copy(*refs, c, part, d).start()

    send_until(1)
    for copy in raw_copies:
        copy.wait()
    for k in (0, 1):
        joined[k, p] = jnp.concatenate([raw[k, 0], raw[k, 1]], axis=1)
    for d in (2, 1, 3):
        vec_copy(d).start()
    send_until(LOOKAHEAD)
    @pl.when(has_right)
    def _():
        pl.semaphore_wait(stage_sem.at[0], 1)

    @pl.when(has_below)
    def _():
        pl.semaphore_wait(stage_sem.at[3], 1)

    @pl.when(col > 0)
    def _():
        signal(stage_sem.at[0], left)

    @pl.when(jnp.logical_and(col == 0, row > 0))
    def _():
        signal(stage_sem.at[3], above)

    @pl.when(me > 0)
    def _():
        pl.semaphore_wait(stage_sem.at[1], 1)

    @pl.when(me == 0)
    def _():
        def answer(n, carry):
            signal(stage_sem.at[1], device_at(0, n, low))
            return carry

        lax.fori_loop(1, groups, answer, 0)

    @pl.when(theirs < mine)
    def _():
        signal(stage_sem.at[2], mirror)
        pl.semaphore_wait(stage_sem.at[2], 1)

    @pl.when(mine < theirs)
    def _():
        pl.semaphore_wait(stage_sem.at[2], 1)
        signal(stage_sem.at[2], mirror)

    acc_p[...] = jnp.zeros_like(acc_p)
    acc_g[...] = jnp.zeros_like(acc_g)
    for copy in rank_copies:
        copy.wait()
    for d in (1, 3, 2):
        vec_arrival(d).wait_recv()
    for k, vec in ((0, vec_w), (1, vec_r)):
        rows = joined[k].reshape(256, 128).astype(jnp.float32).T
        vec[:, :256] = rows.astype(jnp.bfloat16)
        vec[:, 256:] = jnp.concatenate([rows[64:], -rows[:64]], axis=0).astype(jnp.bfloat16)

    def block_copy(send, recv, ssem, rsem, n):
        return pltpu.make_async_remote_copy(
            send.at[n], recv.at[me], ssem.at[n], rsem.at[me],
            device_id=(PANELS * n + q, p), device_id_type=MESH,
        )

    def block_own(send, recv, rsem, n):
        return pltpu.make_async_copy(send.at[n], recv.at[n], rsem.at[n])

    levels = lax.broadcasted_iota(jnp.int32, (1, 128), 1)

    def project(factor, vec, send, recv, ssem, rsem, chunk, column):
        for at in range(0, len(chunk), 2):
            slots = [slot(spot) for spot in chunk[at : at + 2]]
            joint = [factor[place(spot)].reshape(512, 128) for spot in chunk[at : at + 2]]
            joint = joint[0] if len(slots) == 1 else jnp.concatenate(joint, axis=1)
            space = jnp.dot(vec[...], joint, preferred_element_type=jnp.float32)
            for k, n in enumerate(slots):
                other = PANELS * n + q
                if column:
                    rank, here = ranks[other, t], present[other, t]
                else:
                    rank, here = ranks[t, other], present[t, other]
                limit = jnp.where(here == 1, rank, 0)
                part = jnp.where(levels < limit, space[:, 128 * k : 128 * (k + 1)], 0.0)
                send[n] = part.astype(jnp.bfloat16)

                @pl.when(other != t)
                def _():
                    block_copy(send, recv, ssem, rsem, n).start()

                @pl.when(other == t)
                def _():
                    block_own(send, recv, rsem, n).start()

    def expand(factor, recv, rsem, acc, chunk):
        for at in range(0, len(chunk), 2):
            slots = [slot(spot) for spot in chunk[at : at + 2]]
            for n in slots:
                block_own(recv, recv, rsem, n).wait()
            left = [factor[place(spot)].reshape(512, 128) for spot in chunk[at : at + 2]]
            right = [recv[n] for n in slots]
            left = left[0] if len(slots) == 1 else jnp.concatenate(left, axis=1)
            right = right[0] if len(slots) == 1 else jnp.concatenate(right, axis=1)
            acc[...] += lax.dot_general(
                left, right, (((1,), (1,)), ((), ())), preferred_element_type=jnp.float32
            )

    def part_copy(k, d):
        target = (p + d) % PANELS
        return pltpu.make_async_remote_copy(
            part_send.at[k, target], part_recv.at[k, d - 1], p_ssem.at[k, d - 1], p_rsem.at[k, d - 1],
            device_id=(t, target), device_id_type=MESH,
        )

    def send_parts(k, acc):
        lanes = lax.broadcasted_iota(jnp.int32, (256, 128), 1)
        turned = pltpu.roll(acc[256:, :], 64, 1)
        total = acc[:256, :] + jnp.where(lanes < 64, -turned, turned)
        total = total.reshape(PANELS, 64, 128)
        own_sum[k] = total
        part_send[k] = total.astype(jnp.bfloat16)
        for d in (2, 1, 3):
            part_copy(k, d).start()

    def finish(k):
        for d in (1, 3, 2):
            part_copy(k, d).wait_recv()
        total = own_sum[k, p]
        for d in (1, 2, 3):
            total = total + part_recv[k, d - 1].astype(jnp.float32)
        out_ref[k, 0] = total[:, :64].astype(jnp.bfloat16)
        out_ref[k, 1] = total[:, 64:].astype(jnp.bfloat16)

    def arrive(refs, parts):
        for c, part in parts:
            for d in (1, 3, 2):
                factor_arrival(*refs, c, part, d).wait_recv()

    for copy in own_copies:
        copy.wait()
    for c, (kind, chunk, parts) in enumerate(steps):
        arrive(plan[c][0], parts)
        send_until(c + 1 + LOOKAHEAD)
        if kind == "v":
            project(v_all, vec_w, f_send, f_recv, f_ssem, f_rsem, chunk, True)
        else:
            project(u_all, vec_r, a_send, a_recv, a_ssem, a_rsem, chunk, False)
            if len(chunk) > 1:
                expand(u_all, f_recv, f_rsem, acc_p, chunk)
    expand(u_all, f_recv, f_rsem, acc_p, V_CHUNKS[-1])
    send_parts(0, acc_p)
    expand(v_all, a_recv, a_rsem, acc_g, sum((opposite(chunk) for chunk in U_CHUNKS), ()))
    send_parts(1, acc_g)

    for d in (1, 2, 3):
        vec_copy(d).wait_send()
        for refs, parts in plan:
            for c, part in parts:
                factor_copy(*refs, c, part, d).wait_send()

    def settle(n, carry):
        @pl.when(PANELS * n + q != t)
        def _():
            block_copy(f_send, f_recv, f_ssem, f_rsem, n).wait_send()
            block_copy(a_send, a_recv, a_ssem, a_rsem, n).wait_send()

        return carry

    lax.fori_loop(0, groups, settle, 0)
    finish(0)
    finish(1)
    for d in (1, 2, 3):
        for k in (0, 1):
            part_copy(k, d).wait_send()


def on_device(wavefield, residual, v_factors, u_factors, tile_ranks, tile_present):
    tiles = tile_ranks.shape[0]
    groups = tiles // PANELS
    v_local = v_factors.reshape(SIDE, SIDE, PANELS, 2, 64, 128)
    u_local = u_factors.reshape(SIDE, SIDE, PANELS, 2, 64, 128)
    hbm = pl.BlockSpec(memory_space=pl.ANY)
    vmem = pl.BlockSpec(memory_space=pltpu.VMEM)
    b16, f32 = jnp.bfloat16, jnp.float32
    dma = pltpu.SemaphoreType.DMA
    packed = pl.pallas_call(
        functools.partial(kernel, groups),
        out_shape=jax.ShapeDtypeStruct((2, 2, 64, 64), b16),
        in_specs=[hbm] * 6,
        out_specs=vmem,
        scratch_shapes=[
            pltpu.VMEM((2, 2, 64, 64), b16),
            pltpu.VMEM((2, PANELS, 64, 128), b16),
            pltpu.VMEM((128, 512), b16),
            pltpu.VMEM((128, 512), b16),
            pltpu.VMEM((SIDE, SIDE, 2, PANELS, 64, 128), b16),
            pltpu.VMEM((SIDE, SIDE, 2, PANELS, 64, 128), b16),
            pltpu.VMEM((groups, 128, 128), b16),
            pltpu.VMEM((groups, 128, 128), b16),
            pltpu.VMEM((groups, 128, 128), b16),
            pltpu.VMEM((groups, 128, 128), b16),
            pltpu.VMEM((512, 128), f32),
            pltpu.VMEM((512, 128), f32),
            pltpu.VMEM((2, PANELS, 64, 128), f32),
            pltpu.VMEM((2, PANELS, 64, 128), b16),
            pltpu.VMEM((2, 3, 64, 128), b16),
            pltpu.SMEM((tiles, tiles), jnp.int32),
            pltpu.SMEM((tiles, tiles), jnp.int32),
            dma((2,)), dma((2,)), dma((2,)),
            dma((3,)), dma((3,)),
            dma((V_COUNT, 3)), dma((V_COUNT, 3)),
            dma((U_COUNT, 3)), dma((U_COUNT, 3)),
            dma((groups,)), dma((groups,)), dma((groups,)), dma((groups,)),
            dma((2, 3)), dma((2, 3)),
            pltpu.SemaphoreType.REGULAR((4,)),
        ],
        compiler_params=pltpu.CompilerParams(
            collective_id=0, has_side_effects=True, vmem_limit_bytes=32 << 20
        ),
        cost_estimate=pl.CostEstimate(flops=1 << 30, bytes_accessed=4 << 20, transcendentals=0),
    )(*[pltpu.with_memory_space_constraint(x, pltpu.HBM) for x in (wavefield, residual, v_local, u_local, tile_ranks, tile_present)])
    return packed[0], packed[1]


def solution(mesh):
    return jax.shard_map(
        on_device,
        mesh=mesh,
        in_specs=(
            P(None, ("tile", "panel"), None),
            P(None, ("tile", "panel"), None),
            P(None, "tile", None, "panel", None),
            P("tile", None, None, "panel", None),
            P(),
            P(),
        ),
        out_specs=(P(None, ("tile", "panel"), None), P(None, ("tile", "panel"), None)),
        check_vma=False,
    )
```
